32 devices in a mesh: row: 4 (over y, x), col: 8 (over z, core).
Axes of the slice: x: 2, y: 2, z: 4, core: 2. Of those that a mesh axis runs over, the one named last changes fastest.
Arguments:
- l_rows: float32 [4096, 4096], P('row', 'col'), may hold values from -6 to 6
- v_prev: float32 [4096, 1024], P('col', 'row'), may hold values from -0.09375 to 0.09375
- l_tail: float32 [4096, 4096], P('row', 'col'), may hold values from -5 to 100, as said below
- k_cross: float32 [4096, 1024], P('row', 'col'), may hold values from -6 to 6
- k_query: float32 [1024, 1024], P('row', 'col'), may hold values from -2 to 5, as said below
Outputs:
- tail_solution: float32 [4096, 1024], P('row', 'col')
- posterior: float32 [1024, 1024], P('row', 'col')
The draws below stay inside these ranges and needn't reach their ends.
Inputs may be any that keep to these rules, and one draw needn't show every extreme that they name: `l_tail`: lower triangular; its diagonal lies between 40 and 100. `k_query`: symmetric.
All inputs are finite; a program needn't handle non-finite values.
Results may differ from the reference program's by a relative error of at most 0.000076.
Values sent between devices are 32-bit elements; how exact they have to be, the bound alone decides.
A program may use at most 64 MiB of HBM per device.

```python
import math
import jax
import jax.numpy as jnp
from jax import lax

PANEL = 2048
Q = 1024
M = 4096
TAIL = 4096


def draw_l_tail(key, part):
    order = 2 * PANEL
    key_off, key_diag = jax.random.split(jax.random.fold_in(key, 11))
    lower = jnp.clip(1.5 * jax.random.normal(key_off, (order, order), jnp.float32), -5.0, 5.0)
    scales = jnp.exp(jax.random.uniform(key_diag, (order,), jnp.float32, math.log(40.0), math.log(100.0)))
    return jnp.tril(lower, -1) + jnp.diag(scales)


def draw_k_query(key, part):
    key_base = jax.random.fold_in(key, 23)
    spread = 0.3 * jax.random.normal(key_base, (Q, Q), jnp.float32)
    return 0.5 * (spread + spread.T) + 3.0 * jnp.eye(Q, dtype=jnp.float32)


def level_of(stream_key, extent, cuts, smallest, high):
    level, own = 1.0, jax.random.fold_in(stream_key, 6)
    for position, blocks in cuts:
        draws = jnp.exp(jax.random.uniform(jax.random.fold_in(own, position), (blocks,), jnp.float32, smallest / len(cuts), high / len(cuts)))
        level = level * jnp.repeat(draws, extent[position] // blocks).reshape([-1 if axis == position else 1 for axis in range(len(extent))])
    return level


def normal_values(own_key, extent, deviation, reach, shards=(), kind=jnp.bfloat16):
    result = jax.random.normal(own_key, extent, jnp.float32) * deviation
    if len(shards) > 0:
        result = level_of(own_key, extent, shards, -0.22, 0.18) * result
    return jnp.clip(result, min=-reach, max=reach).astype(kind)


def setup_inputs(seed: int = 0) -> dict:
    key_of = jax.random.split(jax.random.key(seed), 6)
    return {
        "l_rows": normal_values(key_of[0], (TAIL, M), 1.0, 6.0, ((0, 4), (1, 8)), jnp.float32),
        "v_prev": normal_values(key_of[1], (M, Q), M ** -0.5, 0.09375, ((0, 8), (1, 4)), jnp.float32),
        "l_tail": draw_l_tail(jax.random.fold_in(key_of[5], 71), 0),
        "k_cross": normal_values(key_of[3], (TAIL, Q), 1.0, 6.0, ((0, 4), (1, 8)), jnp.float32),
        "k_query": draw_k_query(jax.random.fold_in(key_of[5], 71), 0),
    }


def reference(l_rows, v_prev, l_tail, k_cross, k_query):
    highest = lax.Precision.HIGHEST
    residual = k_cross - jnp.dot(l_rows.astype(jnp.float32), v_prev.astype(jnp.float32), precision=highest, preferred_element_type=jnp.float32)
    tail_solution = jax.scipy.linalg.solve_triangular(l_tail, residual, lower=True)
    gram = jnp.dot(v_prev.T.astype(jnp.float32), v_prev.astype(jnp.float32), precision=highest, preferred_element_type=jnp.float32)
    gram = gram + jnp.dot(tail_solution.T.astype(jnp.float32), tail_solution.astype(jnp.float32), precision=highest, preferred_element_type=jnp.float32)
    return (tail_solution, k_query - gram)
```

```python
import functools

import jax
import jax.numpy as jnp
from jax import lax
from jax.experimental import pallas as pl
from jax.experimental.pallas import tpu as pltpu
from jax.sharding import PartitionSpec as P

F32 = jnp.float32
BF16 = jnp.bfloat16
MESH = pl.DeviceIdType.MESH


def split(value):
    high = value.astype(BF16)
    return high, (value - high.astype(F32)).astype(BF16)


def dot3(high, low, value):
    value_high, value_low = split(value)
    total = jnp.dot(high, value_high, preferred_element_type=F32)
    total += jnp.dot(high, value_low, preferred_element_type=F32)
    return total + jnp.dot(low, value_high, preferred_element_type=F32)


def exact_dot(a, b):
    return jnp.dot(a, b, precision=lax.Precision.HIGHEST, preferred_element_type=F32)


def invert_kernel(base, block_ref, out_ref):
    order = block_ref.shape[0]
    rows = lax.broadcasted_iota(jnp.int32, (base, base), 0)
    cols = lax.broadcasted_iota(jnp.int32, (base, base), 1)
    blocks = [block_ref[pl.ds(i, base), pl.ds(i, base)] for i in range(0, order, base)]
    inverses = [jnp.where(rows == cols, 1.0 / block, 0.0) for block in blocks]
    size = 1
    while size < base:
        pair = ((rows // size) % 2 == 1) & (cols // size == rows // size - 1)
        lefts = [exact_dot(inv, jnp.where(pair, block, 0.0)) for inv, block in zip(inverses, blocks)]
        inverses = [inv - exact_dot(left, inv) for inv, left in zip(inverses, lefts)]
        size *= 2
    out_ref[...] = jnp.zeros_like(out_ref)
    for i, inv in enumerate(inverses):
        out_ref[pl.ds(i * base, base), pl.ds(i * base, base)] = inv
    while size < order:
        for i in range(0, order, 2 * size):
            first, second = pl.ds(i, size), pl.ds(i + size, size)
            left = exact_dot(out_ref[second, second], block_ref[second, first])
            out_ref[second, first] = -exact_dot(left, out_ref[first, first])
        size *= 2


def invert(block):
    order = block.shape[0]
    return pl.pallas_call(
        functools.partial(invert_kernel, min(order, 128)),
        out_shape=jax.ShapeDtypeStruct(block.shape, F32),
        in_specs=[pl.BlockSpec(memory_space=pltpu.VMEM)],
        out_specs=pl.BlockSpec(memory_space=pltpu.VMEM),
        compiler_params=pltpu.CompilerParams(vmem_limit_bytes=32 * 2**20),
        cost_estimate=pl.CostEstimate(flops=20 * order**3, bytes_accessed=8 * order * order, transcendentals=0),
    )(block)


def solve_kernel(
    nr, nc, lr_ref, v_ref, lt_ref, inv_ref, kc_ref, out_ref, panel_ref,
    rh, rl, lh, ll, ih, il, s, ex, fin, back, xs, fo, xo,
    ex_s, ex_r, c_s, f_r, b_r, x_s, x_r, o_s, o_r,
):
    r, c = lax.axis_index("row"), lax.axis_index("col")
    h = xs.shape[1]
    z, k = c // 2, c % 2
    planes = nc // 2
    partner = c + 1 - 2 * k
    mine = pl.ds(pl.multiple_of(k * h, h), h)
    other = pl.ds(pl.multiple_of((1 - k) * h, h), h)

    barrier = pltpu.get_barrier_semaphore()

    @pl.loop(1, nr)
    def _(i):
        pl.semaphore_signal(barrier, inc=1, device_id=((r + i) % nr, c), device_id_type=MESH)

    @pl.loop(1, nc)
    def _(i):
        pl.semaphore_signal(barrier, inc=1, device_id=(r, (c + i) % nc), device_id_type=MESH)

    pl.semaphore_wait(barrier, nr + nc - 2)

    def remote(src, dst, send, recv, device):
        return pltpu.make_async_remote_copy(
            src_ref=src, dst_ref=dst, send_sem=send, recv_sem=recv, device_id=device, device_id_type=MESH
        )

    def exchange(q):
        return remote(s.at[q, other], ex.at[q], ex_s.at[q], ex_r.at[q], (r, partner))

    def chain(q, dst, recv, target):
        return remote(fo.at[q], dst.at[q], c_s.at[q], recv.at[q], (r, target))

    def share(i, q):
        return remote(xs.at[q], xs.at[q], x_s.at[i, q], x_r.at[q], ((r + i) % nr, c))

    def deliver(q, target):
        return remote(xs.at[q], xo.at[mine], o_s.at[q], o_r.at[k], (r, target))

    rh[...], rl[...] = split(lr_ref[...])

    @pl.loop(0, nc)
    def _(q):
        s[q] = dot3(rh[...], rl[...], v_ref[q])

        @pl.when(q == c)
        def _():
            s[q] = s[q] - kc_ref[...]

        @pl.when((z > r) | ((z == r) & (k == 1)))
        def _():
            exchange(q).start()

        @pl.when(z > r)
        def _():
            exchange(q).wait_recv()
            fo[q] = s[q, mine] + ex[q]

            @pl.when(z < planes - 1)
            def _():
                chain(q, back, b_r, partner).wait_recv()
                fo[q] = fo[q] + back[q]

            chain(q, back, b_r, c - 2).start()

    @pl.when(z <= r)
    def _():
        lh[...], ll[...] = split(lt_ref[...])

    @pl.when(z == r)
    def _():
        ih[...], il[...] = split(inv_ref[...])

    @pl.loop(0, nc)
    def _(q):
        @pl.when(z < r)
        def _():
            share(1, q).wait_recv()
            s[q] = s[q] + dot3(lh[...], ll[...], xs[q])
            exchange(q).start()
            exchange(q).wait_recv()
            fo[q] = s[q, mine] + ex[q]

            @pl.when(z > 0)
            def _():
                chain(q, fin, f_r, partner).wait_recv()
                fo[q] = fo[q] + fin[q]

            chain(q, fin, f_r, c + 2).start()

        @pl.when(z == r)
        def _():
            exchange(q).wait_recv()
            fo[q] = s[q, mine] + ex[q]

            @pl.when(z > 0)
            def _():
                chain(q, fin, f_r, partner).wait_recv()
                fo[q] = fo[q] + fin[q]

            @pl.when(z < planes - 1)
            def _():
                chain(q, back, b_r, partner).wait_recv()
                fo[q] = fo[q] + back[q]

            xs[q] = dot3(ih[...], il[...], -fo[q])

            @pl.when(k == 0)
            def _():
                s[q, other] = s[q, other] + dot3(lh[h:], ll[h:], xs[q])
                exchange(q).start()

            @pl.loop(1, nr)
            def _(i):
                share(i, q).start()

            @pl.when(q == c)
            def _():
                xo[mine] = xs[q]

            @pl.when(q != c)
            def _():
                deliver(q, q).start()

    @pl.loop(0, nc)
    def _(q):
        exchange(q).wait_send()

        @pl.when(z > r)
        def _():
            share(1, q).wait_recv()

        @pl.when(z != r)
        def _():
            chain(q, fin, f_r, partner).wait_send()

        @pl.when(z == r)
        def _():
            @pl.loop(1, nr)
            def _(i):
                share(i, q).wait_send()

            @pl.when(q != c)
            def _():
                deliver(q, partner).wait_send()

    for half in range(2):
        @pl.when(c != 2 * r + half)
        def _():
            remote(
                xs.at[0], xo.at[pl.ds(half * h, h)], o_s.at[0], o_r.at[half], (r, partner)
            ).wait_recv()

    out_ref[...] = xo[...]
    panel_ref[...] = xs[...]


def body(l_rows, v_prev, l_tail, k_cross, k_query):
    nr, nc = lax.axis_size("row"), lax.axis_size("col")
    tr, tc = l_tail.shape
    tm = l_rows.shape[1]
    w = k_cross.shape[1]
    assert tr == 2 * tc and nc == 2 * nr
    query = w * nc
    r, c = lax.axis_index("row"), lax.axis_index("col")

    v_chunks = v_prev.reshape(tm, nc // nr, w).transpose(1, 0, 2)
    v_all = lax.all_gather(v_chunks, "row", axis=0, tiled=True)
    inverse = invert(lax.dynamic_slice_in_dim(l_tail, (c % 2) * tc, tc, 0))

    vmem = pl.BlockSpec(memory_space=pltpu.VMEM)
    own_block, panel = pl.pallas_call(
        functools.partial(solve_kernel, nr, nc),
        out_shape=(
            jax.ShapeDtypeStruct((tr, w), F32),
            jax.ShapeDtypeStruct((nc, tc, w), F32),
        ),
        in_specs=[vmem] * 5,
        out_specs=(vmem, vmem),
        scratch_shapes=[
            pltpu.VMEM((tr, tm), BF16), pltpu.VMEM((tr, tm), BF16),
            pltpu.VMEM((tr, tc), BF16), pltpu.VMEM((tr, tc), BF16),
            pltpu.VMEM((tc, tc), BF16), pltpu.VMEM((tc, tc), BF16),
            pltpu.VMEM((nc, tr, w), F32),
        ] + [pltpu.VMEM((nc, tc, w), F32)] * 5 + [
            pltpu.VMEM((tr, w), F32),
        ] + [pltpu.SemaphoreType.DMA((nc,))] * 5 + [
            pltpu.SemaphoreType.DMA((nr, nc)),
            pltpu.SemaphoreType.DMA((nc,)),
            pltpu.SemaphoreType.DMA((nc,)),
            pltpu.SemaphoreType.DMA((2,)),
        ],
        compiler_params=pltpu.CompilerParams(
            collective_id=0, has_side_effects=True, vmem_limit_bytes=48 * 2**20
        ),
        cost_estimate=pl.CostEstimate(
            flops=12 * tr * tc * query, bytes_accessed=8 * tr * query, transcendentals=0
        ),
    )(l_rows, v_all, l_tail, inverse, k_cross)

    stacked = jnp.concatenate([v_all, panel], axis=1)
    stacked = stacked.transpose(1, 0, 2).reshape(tm + tc, query)
    rows = query // nr
    left = lax.dynamic_slice_in_dim(stacked, r * rows, rows, 1)
    gram = exact_dot(left.T, stacked)
    gram = lax.psum_scatter(gram, "col", scatter_dimension=1, tiled=True)
    return (own_block, k_query - gram)


def solution(mesh):
    in_specs = (P("row", "col"), P("col", "row"), P("row", "col"), P("row", "col"), P("row", "col"))
    out_specs = (P("row", "col"), P("row", "col"))
    return jax.shard_map(body, mesh=mesh, in_specs=in_specs, out_specs=out_specs, check_vma=False)
```

```python
import functools

import jax
import jax.numpy as jnp
from jax import lax
from jax.experimental import pallas as pl
from jax.experimental.pallas import tpu as pltpu
from jax.sharding import PartitionSpec as P

F32 = jnp.float32
BF16 = jnp.bfloat16
MESH = pl.DeviceIdType.MESH


def split(value):
    high = value.astype(BF16)
    return high, (value - high.astype(F32)).astype(BF16)


def dot3(high, low, value):
    value_high, value_low = split(value)
    total = jnp.dot(high, value_high, preferred_element_type=F32)
    total += jnp.dot(high, value_low, preferred_element_type=F32)
    return total + jnp.dot(low, value_high, preferred_element_type=F32)


def start(copy):
    copy.start()


def wait_send(copy):
    copy.wait_send()


def grid_of(count):
    side = max(i for i in range(1, count + 1) if count % i == 0 and i * i <= count)
    return side, count // side


def exact_dot(a, b):
    return jnp.dot(a, b, precision=lax.Precision.HIGHEST, preferred_element_type=F32)


def invert(base, block_ref, out_ref):
    order = out_ref.shape[0]
    rows = lax.broadcasted_iota(jnp.int32, (base, base), 0)
    cols = lax.broadcasted_iota(jnp.int32, (base, base), 1)
    blocks = [block_ref[pl.ds(i, base), pl.ds(i, base)] for i in range(0, order, base)]
    inverses = [jnp.where(rows == cols, 1.0 / block, 0.0) for block in blocks]
    size = 1
    while size < base:
        pair = ((rows // size) % 2 == 1) & (cols // size == rows // size - 1)
        lefts = [exact_dot(inv, jnp.where(pair, block, 0.0)) for inv, block in zip(inverses, blocks)]
        inverses = [inv - exact_dot(left, inv) for inv, left in zip(inverses, lefts)]
        size *= 2
    out_ref[...] = jnp.zeros_like(out_ref)
    for i, inv in enumerate(inverses):
        out_ref[pl.ds(i * base, base), pl.ds(i * base, base)] = inv
    while size < order:
        for i in range(0, order, 2 * size):
            first, second = pl.ds(i, size), pl.ds(i + size, size)
            left = exact_dot(out_ref[second, second], block_ref[second, first])
            out_ref[second, first] = -exact_dot(left, out_ref[first, first])
        size *= 2


def solve_kernel(
    nr, nc, lr_ref, v_ref, lt_ref, kc_ref, out_ref, panel_ref, v_out_ref,
    rh, rl, lh, ll, inv, ih, il, s, ex, fin, back, xs, fo, vs, xo,
    ex_s, ex_r, c_s, f_r, b_r, o_s, o_r, x_s, x_r, v_s, v_r,
):
    r, c = lax.axis_index("row"), lax.axis_index("col")
    h = xs.shape[1]
    z, k = c // 2, c % 2
    planes = nc // 2
    partner = c + 1 - 2 * k
    mine = pl.ds(pl.multiple_of(k * h, h), h)
    other = pl.ds(pl.multiple_of((1 - k) * h, h), h)

    barrier = pltpu.get_barrier_semaphore()

    @pl.loop(1, nr)
    def _(i):
        pl.semaphore_signal(barrier, inc=1, device_id=((r + i) % nr, c), device_id_type=MESH)

    @pl.loop(1, nc)
    def _(i):
        pl.semaphore_signal(barrier, inc=1, device_id=(r, (c + i) % nc), device_id_type=MESH)

    pl.semaphore_wait(barrier, nr + nc - 2)

    def remote(src, dst, send, recv, device):
        return pltpu.make_async_remote_copy(
            src_ref=src, dst_ref=dst, send_sem=send, recv_sem=recv, device_id=device, device_id_type=MESH
        )

    def exchange(q):
        return remote(s.at[q, other], ex.at[q], ex_s.at[q], ex_r.at[q], (r, partner))

    def chain(q, dst, recv, target):
        return remote(fo.at[q], dst.at[q], c_s.at[q], recv.at[q], (r, target))

    ga, gb = grid_of(nr)
    a, b = r // gb, r % gb

    def halves(buf, sends, recvs, q, half, along, i):
        rows = buf.shape[1] // 2
        part = pl.ds(half * rows, rows)
        row, slot = (a * gb + (b + i) % gb, i - 1) if along else (((a + i) % ga) * gb + b, gb - 2 + i)
        return remote(
            buf.at[q, part], buf.at[q, part], sends.at[slot, half, q], recvs.at[half, q], (row, c)
        )

    def from_source(group, q, act):
        for half in range(2):
            for i in range(1, gb):
                act(halves(*group, q, half, True, i))
            for i in range(1, ga):
                act(halves(*group, q, 1 - half, False, i))

    def pass_on(group, q, half, act):
        for i in range(1, gb if half else ga):
            act(halves(*group, q, half, bool(half), i))

    def arrived(group, q, half):
        halves(*group, q, half, gb > 1, 1).wait_recv()

    def receive(group, q, src):
        @pl.when((a == src // gb) & (b != src % gb))
        def _():
            arrived(group, q, 0)
            pass_on(group, q, 0, start)
            arrived(group, q, 1)

        @pl.when((a != src // gb) & (b == src % gb))
        def _():
            arrived(group, q, 1)
            pass_on(group, q, 1, start)
            arrived(group, q, 0)

        @pl.when((a != src // gb) & (b != src % gb))
        def _():
            arrived(group, q, 0)
            arrived(group, q, 1)

    def sent(group, q, src):
        @pl.when(r == src)
        def _():
            from_source(group, q, wait_send)

        @pl.when((a == src // gb) & (b != src % gb))
        def _():
            pass_on(group, q, 0, wait_send)

        @pl.when((a != src // gb) & (b == src % gb))
        def _():
            pass_on(group, q, 1, wait_send)

    solved, prior = (xs, x_s, x_r), (vs, v_s, v_r)
    per = nc // nr

    def turn(t):
        return (t % nr) * per + t // nr

    def deliver(q, target):
        return remote(xs.at[q], xo.at[mine], o_s.at[q], o_r.at[k], (r, target))

    for i in range(per):
        vs[r * per + i] = v_ref[i]
        from_source(prior, r * per + i, start)

    rh[...], rl[...] = split(lr_ref[...])

    @pl.when(z <= r)
    def _():
        lh[...], ll[...] = split(lt_ref[...])

    @pl.when(z == r)
    def _():
        for half in range(2):
            @pl.when(k == half)
            def _():
                invert(min(h, 128), lt_ref.at[pl.ds(half * h, h)], inv)

        ih[...], il[...] = split(inv[...])

    @pl.loop(0, nc)
    def _(t):
        q = turn(t)
        receive(prior, q, q // per)
        s[q] = dot3(rh[...], rl[...], vs[q])

        @pl.when(q == c)
        def _():
            s[q] = s[q] - kc_ref[...]

        @pl.when((z > r) | ((z == r) & (k == 1)))
        def _():
            exchange(q).start()

        @pl.when(z > r)
        def _():
            exchange(q).wait_recv()
            fo[q] = s[q, mine] + ex[q]

            @pl.when(z < planes - 1)
            def _():
                chain(q, back, b_r, partner).wait_recv()
                fo[q] = fo[q] + back[q]

            chain(q, back, b_r, c - 2).start()

    @pl.loop(0, nc)
    def _(t):
        q = turn(t)
        receive(solved, q, z)

        @pl.when(z < r)
        def _():
            s[q] = s[q] + dot3(lh[...], ll[...], xs[q])
            exchange(q).start()
            exchange(q).wait_recv()
            fo[q] = s[q, mine] + ex[q]

            @pl.when(z > 0)
            def _():
                chain(q, fin, f_r, partner).wait_recv()
                fo[q] = fo[q] + fin[q]

            chain(q, fin, f_r, c + 2).start()

        @pl.when(z == r)
        def _():
            exchange(q).wait_recv()
            fo[q] = s[q, mine] + ex[q]

            @pl.when(z > 0)
            def _():
                chain(q, fin, f_r, partner).wait_recv()
                fo[q] = fo[q] + fin[q]

            @pl.when(z < planes - 1)
            def _():
                chain(q, back, b_r, partner).wait_recv()
                fo[q] = fo[q] + back[q]

            xs[q] = dot3(ih[...], il[...], -fo[q])

            from_source(solved, q, start)

            @pl.when(k == 0)
            def _():
                s[q, other] = s[q, other] + dot3(lh[h:], ll[h:], xs[q])
                exchange(q).start()

            @pl.when(q == c)
            def _():
                xo[mine] = xs[q]

            @pl.when(q != c)
            def _():
                deliver(q, q).start()

    @pl.loop(0, nc)
    def _(q):
        exchange(q).wait_send()

        sent(prior, q, q // per)
        sent(solved, q, z)

        @pl.when(z != r)
        def _():
            chain(q, fin, f_r, partner).wait_send()

        @pl.when(z == r)
        def _():
            @pl.when(q != c)
            def _():
                deliver(q, partner).wait_send()

    for half in range(2):
        @pl.when(c != 2 * r + half)
        def _():
            remote(
                xs.at[0], xo.at[pl.ds(half * h, h)], o_s.at[0], o_r.at[half], (r, partner)
            ).wait_recv()

    out_ref[...] = xo[...]
    panel_ref[...] = xs[...]
    v_out_ref[...] = vs[...]


def body(l_rows, v_prev, l_tail, k_cross, k_query):
    nr, nc = lax.axis_size("row"), lax.axis_size("col")
    tr, tc = l_tail.shape
    tm = l_rows.shape[1]
    w = k_cross.shape[1]
    assert tr == 2 * tc and nc == 2 * nr
    query = w * nc
    r = lax.axis_index("row")
    slots = sum(grid_of(nr)) - 2

    v_chunks = v_prev.reshape(tm, nc // nr, w).transpose(1, 0, 2)

    vmem = pl.BlockSpec(memory_space=pltpu.VMEM)
    own_block, panel, v_all = pl.pallas_call(
        functools.partial(solve_kernel, nr, nc),
        out_shape=(
            jax.ShapeDtypeStruct((tr, w), F32),
            jax.ShapeDtypeStruct((nc, tc, w), F32),
            jax.ShapeDtypeStruct((nc, tm, w), F32),
        ),
        in_specs=[vmem] * 4,
        out_specs=(vmem, vmem, vmem),
        scratch_shapes=[
            pltpu.VMEM((tr, tm), BF16), pltpu.VMEM((tr, tm), BF16),
            pltpu.VMEM((tr, tc), BF16), pltpu.VMEM((tr, tc), BF16),
            pltpu.VMEM((tc, tc), F32),
            pltpu.VMEM((tc, tc), BF16), pltpu.VMEM((tc, tc), BF16),
            pltpu.VMEM((nc, tr, w), F32),
        ] + [pltpu.VMEM((nc, tc, w), F32)] * 5 + [
            pltpu.VMEM((nc, tm, w), F32),
            pltpu.VMEM((tr, w), F32),
        ] + [pltpu.SemaphoreType.DMA((nc,))] * 6 + [
            pltpu.SemaphoreType.DMA((2,)),
        ] + [
            pltpu.SemaphoreType.DMA((slots, 2, nc)), pltpu.SemaphoreType.DMA((2, nc)),
        ] * 2,
        compiler_params=pltpu.CompilerParams(
            collective_id=0, has_side_effects=True, vmem_limit_bytes=48 * 2**20
        ),
        cost_estimate=pl.CostEstimate(
            flops=12 * tr * tc * query, bytes_accessed=8 * tr * query, transcendentals=0
        ),
    )(l_rows, v_chunks, l_tail, k_cross)

    stacked = jnp.concatenate([v_all, panel], axis=1)
    stacked = stacked.transpose(1, 0, 2).reshape(tm + tc, query)
    rows = query // nr
    left = lax.dynamic_slice_in_dim(stacked, r * rows, rows, 1)
    gram = exact_dot(left.T, stacked)
    gram = lax.psum_scatter(gram, "col", scatter_dimension=1, tiled=True)
    return (own_block, k_query - gram)


def solution(mesh):
    in_specs = (P("row", "col"), P("col", "row"), P("row", "col"), P("row", "col"), P("row", "col"))
    out_specs = (P("row", "col"), P("row", "col"))
    return jax.shard_map(body, mesh=mesh, in_specs=in_specs, out_specs=out_specs, check_vma=False)
```

```python
import functools

import jax
import jax.numpy as jnp
from jax import lax
from jax.experimental import pallas as pl
from jax.experimental.pallas import tpu as pltpu
from jax.sharding import PartitionSpec as P

F32 = jnp.float32
BF16 = jnp.bfloat16
MESH = pl.DeviceIdType.MESH


def split(value):
    high = value.astype(BF16)
    return high, (value - high.astype(F32)).astype(BF16)


def dot3(high, low, value):
    value_high, value_low = split(value)
    total = jnp.dot(high, value_high, preferred_element_type=F32)
    total += jnp.dot(high, value_low, preferred_element_type=F32)
    return total + jnp.dot(low, value_high, preferred_element_type=F32)


def start(copy):
    copy.start()


def wait_send(copy):
    copy.wait_send()


def grid_of(count):
    side = max(i for i in range(1, count + 1) if count % i == 0 and i * i <= count)
    return side, count // side


def exact_dot(a, b):
    return jnp.dot(a, b, precision=lax.Precision.HIGHEST, preferred_element_type=F32)


def invert(base, block_ref, out_ref):
    order = out_ref.shape[0]
    rows = lax.broadcasted_iota(jnp.int32, (base, base), 0)
    cols = lax.broadcasted_iota(jnp.int32, (base, base), 1)
    blocks = [block_ref[pl.ds(i, base), pl.ds(i, base)] for i in range(0, order, base)]
    inverses = [jnp.where(rows == cols, 1.0 / block, 0.0) for block in blocks]
    size = 1
    while size < base:
        pair = ((rows // size) % 2 == 1) & (cols // size == rows // size - 1)
        lefts = [exact_dot(inv, jnp.where(pair, block, 0.0)) for inv, block in zip(inverses, blocks)]
        inverses = [inv - exact_dot(left, inv) for inv, left in zip(inverses, lefts)]
        size *= 2
    out_ref[...] = jnp.zeros_like(out_ref)
    for i, inv in enumerate(inverses):
        out_ref[pl.ds(i * base, base), pl.ds(i * base, base)] = inv
    while size < order:
        for i in range(0, order, 2 * size):
            first, second = pl.ds(i, size), pl.ds(i + size, size)
            left = exact_dot(out_ref[second, second], block_ref[second, first])
            out_ref[second, first] = -exact_dot(left, out_ref[first, first])
        size *= 2


def solve_kernel(
    nr, nc, lr_ref, v_ref, lt_ref, kc_ref, kq_ref, out_ref, post_ref,
    rh, rl, lh, ll, inv, ih, il, th, tl, yh, yl, s, ex, fin, back, xs, fo, vs, xo, g, gx, gin,
    ex_s, ex_r, c_s, f_r, b_r, o_s, o_r, x_s, x_r, v_s, v_r, gx_s, gx_r, g_s, g_r,
):
    r, c = lax.axis_index("row"), lax.axis_index("col")
    h = xs.shape[1]
    z, k = c // 2, c % 2
    planes = nc // 2
    partner = c + 1 - 2 * k
    mine = pl.ds(pl.multiple_of(k * h, h), h)
    other = pl.ds(pl.multiple_of((1 - k) * h, h), h)

    barrier = pltpu.get_barrier_semaphore()

    @pl.loop(1, nr)
    def _(i):
        pl.semaphore_signal(barrier, inc=1, device_id=((r + i) % nr, c), device_id_type=MESH)

    @pl.loop(1, nc)
    def _(i):
        pl.semaphore_signal(barrier, inc=1, device_id=(r, (c + i) % nc), device_id_type=MESH)

    pl.semaphore_wait(barrier, nr + nc - 2)

    def remote(src, dst, send, recv, device):
        return pltpu.make_async_remote_copy(
            src_ref=src, dst_ref=dst, send_sem=send, recv_sem=recv, device_id=device, device_id_type=MESH
        )

    def exchange(q):
        return remote(s.at[q, other], ex.at[q], ex_s.at[q], ex_r.at[q], (r, partner))

    def chain(q, dst, recv, target):
        return remote(fo.at[q], dst.at[q], c_s.at[q], recv.at[q], (r, target))

    ga, gb = grid_of(nr)
    a, b = r // gb, r % gb

    def halves(buf, sends, recvs, q, half, along, i):
        rows = buf.shape[1] // 2
        part = pl.ds(half * rows, rows)
        row, slot = (a * gb + (b + i) % gb, i - 1) if along else (((a + i) % ga) * gb + b, gb - 2 + i)
        return remote(
            buf.at[q, part], buf.at[q, part], sends.at[slot, half, q], recvs.at[half, q], (row, c)
        )

    def from_source(group, q, act):
        for half in range(2):
            for i in range(1, gb):
                act(halves(*group, q, half, True, i))
            for i in range(1, ga):
                act(halves(*group, q, 1 - half, False, i))

    def pass_on(group, q, half, act):
        for i in range(1, gb if half else ga):
            act(halves(*group, q, half, bool(half), i))

    def arrived(group, q, half):
        halves(*group, q, half, gb > 1, 1).wait_recv()

    def receive(group, q, src):
        @pl.when((a == src // gb) & (b != src % gb))
        def _():
            arrived(group, q, 0)
            pass_on(group, q, 0, start)
            arrived(group, q, 1)

        @pl.when((a != src // gb) & (b == src % gb))
        def _():
            arrived(group, q, 1)
            pass_on(group, q, 1, start)
            arrived(group, q, 0)

        @pl.when((a != src // gb) & (b != src % gb))
        def _():
            arrived(group, q, 0)
            arrived(group, q, 1)

    def sent(group, q, src):
        @pl.when(r == src)
        def _():
            from_source(group, q, wait_send)

        @pl.when((a == src // gb) & (b != src % gb))
        def _():
            pass_on(group, q, 0, wait_send)

        @pl.when((a != src // gb) & (b == src % gb))
        def _():
            pass_on(group, q, 1, wait_send)

    solved, prior = (xs, x_s, x_r), (vs, v_s, v_r)
    per = nc // nr

    def turn(t):
        return (t % nr) * per + t // nr

    def deliver(q, target):
        return remote(xs.at[q], xo.at[mine], o_s.at[q], o_r.at[k], (r, target))

    def pair_up(target):
        return remote(
            g.at[2 * target + 1 - k], gx.at[target], gx_s.at[target], gx_r.at[target], (r, partner)
        )

    def scatter(target, slot):
        return remote(
            g.at[2 * target + k], gin.at[slot], g_s.at[target], g_r.at[slot], (r, 2 * target + k)
        )

    def transposed(chunks):
        return split(jnp.concatenate([chunks[r * per + i].T for i in range(per)], axis=0))

    w = kc_ref.shape[1]
    for i in range(per):
        vs[r * per + i] = v_ref[:, i * w:(i + 1) * w]
        from_source(prior, r * per + i, start)

    rh[...], rl[...] = split(lr_ref[...])

    @pl.when(z <= r)
    def _():
        lh[...], ll[...] = split(lt_ref[...])

    @pl.when(z == r)
    def _():
        for half in range(2):
            @pl.when(k == half)
            def _():
                invert(min(h, 128), lt_ref.at[pl.ds(half * h, h)], inv)

        ih[...], il[...] = split(inv[...])

    th[...], tl[...] = transposed(vs)

    @pl.loop(0, nc)
    def _(t):
        q = turn(t)
        receive(prior, q, q // per)
        s[q] = dot3(rh[...], rl[...], vs[q])

        @pl.when(q == c)
        def _():
            s[q] = s[q] - kc_ref[...]

        @pl.when((z > r) | ((z == r) & (k == 1)))
        def _():
            exchange(q).start()

        @pl.when(z > r)
        def _():
            exchange(q).wait_recv()
            fo[q] = s[q, mine] + ex[q]

            @pl.when(z < planes - 1)
            def _():
                chain(q, back, b_r, partner).wait_recv()
                fo[q] = fo[q] + back[q]

            chain(q, back, b_r, c - 2).start()

        g[q] = dot3(th[...], tl[...], vs[q])

    @pl.loop(0, nc)
    def _(t):
        q = turn(t)
        receive(solved, q, z)

        @pl.when(z < r)
        def _():
            s[q] = s[q] + dot3(lh[...], ll[...], xs[q])
            exchange(q).start()
            exchange(q).wait_recv()
            fo[q] = s[q, mine] + ex[q]

            @pl.when(z > 0)
            def _():
                chain(q, fin, f_r, partner).wait_recv()
                fo[q] = fo[q] + fin[q]

            chain(q, fin, f_r, c + 2).start()

        @pl.when(z == r)
        def _():
            exchange(q).wait_recv()
            fo[q] = s[q, mine] + ex[q]

            @pl.when(z > 0)
            def _():
                chain(q, fin, f_r, partner).wait_recv()
                fo[q] = fo[q] + fin[q]

            @pl.when(z < planes - 1)
            def _():
                chain(q, back, b_r, partner).wait_recv()
                fo[q] = fo[q] + back[q]

            xs[q] = dot3(ih[...], il[...], -fo[q])

            from_source(solved, q, start)

            @pl.when(k == 0)
            def _():
                s[q, other] = s[q, other] + dot3(lh[h:], ll[h:], xs[q])
                exchange(q).start()

            @pl.when(q == c)
            def _():
                xo[mine] = xs[q]

            @pl.when(q != c)
            def _():
                deliver(q, q).start()

    yh[...], yl[...] = transposed(xs)

    @pl.loop(0, planes)
    def _(i):
        target = (z + 1 + i) % planes
        away, home = 2 * target + 1 - k, 2 * target + k
        g[away] = g[away] + dot3(yh[...], yl[...], xs[away])
        pair_up(target).start()
        g[home] = g[home] + dot3(yh[...], yl[...], xs[home])

    @pl.loop(0, planes)
    def _(i):
        target = (z + 1 + i) % planes
        pair_up(target).wait_recv()
        g[2 * target + k] = g[2 * target + k] + gx[target]

        @pl.when(target != z)
        def _():
            scatter(target, z).start()

    @pl.loop(0, nc)
    def _(q):
        exchange(q).wait_send()

        sent(prior, q, q // per)
        sent(solved, q, z)

        @pl.when(z != r)
        def _():
            chain(q, fin, f_r, partner).wait_send()

        @pl.when(z == r)
        def _():
            @pl.when(q != c)
            def _():
                deliver(q, partner).wait_send()

    for half in range(2):
        @pl.when(c != 2 * r + half)
        def _():
            remote(
                xs.at[0], xo.at[pl.ds(half * h, h)], o_s.at[0], o_r.at[half], (r, partner)
            ).wait_recv()

    out_ref[...] = xo[...]
    post_ref[...] = kq_ref[...] - g[c]

    @pl.loop(0, planes)
    def _(i):
        pair_up(i).wait_send()

        @pl.when(i != z)
        def _():
            scatter(i, z).wait_send()
            scatter((z + 1) % planes, i).wait_recv()
            post_ref[...] = post_ref[...] - gin[i]


def body(l_rows, v_prev, l_tail, k_cross, k_query):
    nr, nc = lax.axis_size("row"), lax.axis_size("col")
    tr, tc = l_tail.shape
    tm = l_rows.shape[1]
    w = k_cross.shape[1]
    assert tr == 2 * tc and nc == 2 * nr
    query = w * nc
    slots = sum(grid_of(nr)) - 2
    planes, rows = nc // 2, query // nr

    vmem = pl.BlockSpec(memory_space=pltpu.VMEM)
    return pl.pallas_call(
        functools.partial(solve_kernel, nr, nc),
        out_shape=(
            jax.ShapeDtypeStruct((tr, w), F32),
            jax.ShapeDtypeStruct(k_query.shape, F32),
        ),
        in_specs=[vmem] * 5,
        out_specs=(vmem, vmem),
        scratch_shapes=[
            pltpu.VMEM((tr, tm), BF16), pltpu.VMEM((tr, tm), BF16),
            pltpu.VMEM((tr, tc), BF16), pltpu.VMEM((tr, tc), BF16),
            pltpu.VMEM((tc, tc), F32),
            pltpu.VMEM((tc, tc), BF16), pltpu.VMEM((tc, tc), BF16),
            pltpu.VMEM((rows, tm), BF16), pltpu.VMEM((rows, tm), BF16),
            pltpu.VMEM((rows, tc), BF16), pltpu.VMEM((rows, tc), BF16),
            pltpu.VMEM((nc, tr, w), F32),
        ] + [pltpu.VMEM((nc, tc, w), F32)] * 5 + [
            pltpu.VMEM((nc, tm, w), F32),
            pltpu.VMEM((tr, w), F32),
            pltpu.VMEM((nc, rows, w), F32),
            pltpu.VMEM((planes, rows, w), F32),
            pltpu.VMEM((planes, rows, w), F32),
        ] + [pltpu.SemaphoreType.DMA((nc,))] * 6 + [
            pltpu.SemaphoreType.DMA((2,)),
        ] + [
            pltpu.SemaphoreType.DMA((slots, 2, nc)), pltpu.SemaphoreType.DMA((2, nc)),
        ] * 2 + [pltpu.SemaphoreType.DMA((planes,))] * 4,
        compiler_params=pltpu.CompilerParams(
            collective_id=0, has_side_effects=True, vmem_limit_bytes=48 * 2**20
        ),
        cost_estimate=pl.CostEstimate(
            flops=12 * tr * tc * query, bytes_accessed=8 * tr * query, transcendentals=0
        ),
    )(l_rows, v_prev, l_tail, k_cross, k_query)


def solution(mesh):
    in_specs = (P("row", "col"), P("col", "row"), P("row", "col"), P("row", "col"), P("row", "col"))
    out_specs = (P("row", "col"), P("row", "col"))
    return jax.shard_map(body, mesh=mesh, in_specs=in_specs, out_specs=out_specs, check_vma=False)
```

```python
import functools

import jax
import jax.numpy as jnp
from jax import lax
from jax.experimental import pallas as pl
from jax.experimental.pallas import tpu as pltpu
from jax.sharding import PartitionSpec as P

F32 = jnp.float32
BF16 = jnp.bfloat16
MESH = pl.DeviceIdType.MESH


def split(value):
    high = value.astype(BF16)
    return high, (value - high.astype(F32)).astype(BF16)


def dot3(high, low, value):
    value_high, value_low = split(value)
    total = jnp.dot(high, value_high, preferred_element_type=F32)
    total += jnp.dot(high, value_low, preferred_element_type=F32)
    return total + jnp.dot(low, value_high, preferred_element_type=F32)


def start(copy):
    copy.start()


def wait_send(copy):
    copy.wait_send()


def grid_of(count):
    side = max(i for i in range(1, count + 1) if count % i == 0 and i * i <= count)
    return side, count // side


def exact_dot(a, b):
    return jnp.dot(a, b, precision=lax.Precision.HIGHEST, preferred_element_type=F32)


def invert(base, block_ref, out_ref):
    order = out_ref.shape[0]
    rows = lax.broadcasted_iota(jnp.int32, (base, base), 0)
    cols = lax.broadcasted_iota(jnp.int32, (base, base), 1)
    blocks = [block_ref[pl.ds(i, base), pl.ds(i, base)] for i in range(0, order, base)]
    inverses = [jnp.where(rows == cols, 1.0 / block, 0.0) for block in blocks]
    size = 1
    while size < base:
        pair = ((rows // size) % 2 == 1) & (cols // size == rows // size - 1)
        lefts = [exact_dot(inv, jnp.where(pair, block, 0.0)) for inv, block in zip(inverses, blocks)]
        inverses = [inv - exact_dot(left, inv) for inv, left in zip(inverses, lefts)]
        size *= 2
    out_ref[...] = jnp.zeros_like(out_ref)
    for i, inv in enumerate(inverses):
        out_ref[pl.ds(i * base, base), pl.ds(i * base, base)] = inv
    while size < order:
        for i in range(0, order, 2 * size):
            first, second = pl.ds(i, size), pl.ds(i + size, size)
            left = exact_dot(out_ref[second, second], block_ref[second, first])
            out_ref[second, first] = -exact_dot(left, out_ref[first, first])
        size *= 2


def solve_kernel(
    nr, nc, lr_hbm, v_hbm, lt_hbm, kc_hbm, kq_hbm, out_ref, post_ref,
    lr_ref, v_ref, lt_ref, kc_ref, kq_ref,
    rh, rl, lh, ll, inv, ih, il, th, tl, yh, yl, s, ex, fin, back, xs, fo, vs, xo, g, gx, gin,
    ex_s, ex_r, c_s, f_r, b_r, o_s, o_r, x_s, x_r, v_s, v_r, gx_s, gx_r, g_s, g_r, load_s,
):
    r, c = lax.axis_index("row"), lax.axis_index("col")
    h = xs.shape[1]
    z, k = c // 2, c % 2
    planes = nc // 2
    partner = c + 1 - 2 * k
    mine = pl.ds(pl.multiple_of(k * h, h), h)
    hh = h // 2
    pieces = [pl.ds(i * hh, hh) for i in range(2)]

    def rows_of(half, p):
        return pl.ds(pl.multiple_of(half * h + p * hh, hh), hh)

    loads = [
        pltpu.make_async_copy(src, dst, load_s.at[i])
        for i, (src, dst) in enumerate([
            (v_hbm, v_ref), (lr_hbm, lr_ref), (kc_hbm, kc_ref), (lt_hbm, lt_ref), (kq_hbm, kq_ref)
        ])
    ]
    for load in loads:
        load.start()

    barrier = pltpu.get_barrier_semaphore()

    @pl.loop(1, nr)
    def _(i):
        pl.semaphore_signal(barrier, inc=1, device_id=((r + i) % nr, c), device_id_type=MESH)

    @pl.loop(1, nc)
    def _(i):
        pl.semaphore_signal(barrier, inc=1, device_id=(r, (c + i) % nc), device_id_type=MESH)

    pl.semaphore_wait(barrier, nr + nc - 2)

    def remote(src, dst, send, recv, device):
        return pltpu.make_async_remote_copy(
            src_ref=src, dst_ref=dst, send_sem=send, recv_sem=recv, device_id=device, device_id_type=MESH
        )

    def exchange(q, p):
        return remote(
            s.at[q, rows_of(1 - k, p)], ex.at[q, pieces[p]], ex_s.at[p, q], ex_r.at[p, q], (r, partner)
        )

    def chain(q, p, dst, recv, target):
        return remote(
            fo.at[q, pieces[p]], dst.at[q, pieces[p]], c_s.at[p, q], recv.at[p, q], (r, target)
        )

    def gather_piece(q, p):
        exchange(q, p).wait_recv()
        fo[q, pieces[p]] = s[q, rows_of(k, p)] + ex[q, pieces[p]]

    def add_from(q, p, dst, recv, there):
        @pl.when(there)
        def _():
            chain(q, p, dst, recv, partner).wait_recv()
            fo[q, pieces[p]] = fo[q, pieces[p]] + dst[q, pieces[p]]

    ga, gb = grid_of(nr)
    a, b = r // gb, r % gb

    def halves(buf, sends, recvs, q, half, along, i):
        rows = buf.shape[1] // 2
        part = pl.ds(half * rows, rows)
        row, slot = (a * gb + (b + i) % gb, i - 1) if along else (((a + i) % ga) * gb + b, gb - 2 + i)
        return remote(
            buf.at[q, part], buf.at[q, part], sends.at[slot, half, q], recvs.at[half, q], (row, c)
        )

    def from_source(group, q, act, part=(0, 1)):
        for half in part:
            for i in range(1, gb):
                act(halves(*group, q, half, True, i))
            for i in range(1, ga):
                act(halves(*group, q, half, False, i))

    def pass_on(group, q, half, act):
        for i in range(1, gb if half else ga):
            act(halves(*group, q, half, bool(half), i))

    def arrived(group, q, half):
        halves(*group, q, half, gb > 1, 1).wait_recv()

    def receive(group, q, src):
        @pl.when((a == src // gb) & (b != src % gb))
        def _():
            arrived(group, q, 0)
            pass_on(group, q, 0, start)
            arrived(group, q, 1)

        @pl.when((a != src // gb) & (b == src % gb))
        def _():
            arrived(group, q, 1)
            pass_on(group, q, 1, start)
            arrived(group, q, 0)

        @pl.when((a != src // gb) & (b != src % gb))
        def _():
            arrived(group, q, 0)
            arrived(group, q, 1)

    def sent(group, q, src):
        @pl.when(r == src)
        def _():
            from_source(group, q, wait_send)

        @pl.when((a == src // gb) & (b != src % gb))
        def _():
            pass_on(group, q, 0, wait_send)

        @pl.when((a != src // gb) & (b == src % gb))
        def _():
            pass_on(group, q, 1, wait_send)

    solved, prior = (xs, x_s, x_r), (vs, v_s, v_r)
    per = nc // nr

    def turn(t):
        return (t % nr) * per + t // nr

    def deliver(q, target):
        return remote(xs.at[q], xo.at[mine], o_s.at[q], o_r.at[k], (r, target))

    def pair_up(target):
        return remote(
            g.at[2 * target + 1 - k], gx.at[target], gx_s.at[target], gx_r.at[target], (r, partner)
        )

    def scatter(target, slot):
        return remote(
            g.at[2 * target + k], gin.at[slot], g_s.at[target], g_r.at[slot], (r, 2 * target + k)
        )

    def transposed(chunks):
        return split(jnp.concatenate([chunks[r * per + i].T for i in range(per)], axis=0))

    w = kc_ref.shape[1]
    loads[0].wait()
    for i in range(per):
        vs[r * per + i] = v_ref[:, i * w:(i + 1) * w]
        from_source(prior, r * per + i, start)

    loads[1].wait()
    rh[...], rl[...] = split(lr_ref[...])
    th[...], tl[...] = transposed(vs)
    loads[2].wait()

    @pl.loop(0, nc)
    def _(t):
        q = turn(t)
        receive(prior, q, q // per)

        def update(half, p):
            rows = rows_of(half, p)
            term = dot3(rh[rows], rl[rows], vs[q])
            s[q, rows] = term - jnp.where(q == c, kc_ref[rows], 0.0)

        for p in range(2):
            update(1 - k, p)

            @pl.when((z > r) | ((z == r) & (k == 1)))
            def _():
                exchange(q, p).start()

        for p in range(2):
            update(k, p)

            @pl.when(z > r)
            def _():
                gather_piece(q, p)
                add_from(q, p, back, b_r, z < planes - 1)
                chain(q, p, back, b_r, c - 2).start()

        g[q] = dot3(th[...], tl[...], vs[q])

    loads[3].wait()

    @pl.when(z <= r)
    def _():
        lh[...], ll[...] = split(lt_ref[...])

    @pl.when(z == r)
    def _():
        for half in range(2):
            @pl.when(k == half)
            def _():
                invert(min(h, 128), lt_ref.at[pl.ds(half * h, h)], inv)

        ih[...], il[...] = split(inv[...])

    @pl.loop(0, nc)
    def _(t):
        q = turn(t)
        receive(solved, q, z)

        @pl.when(z < r)
        def _():
            def update(half, p):
                rows = rows_of(half, p)
                s[q, rows] = s[q, rows] + dot3(lh[rows], ll[rows], xs[q])

            for p in range(2):
                update(1 - k, p)
                exchange(q, p).start()

            for p in range(2):
                update(k, p)
                gather_piece(q, p)
                add_from(q, p, fin, f_r, z > 0)
                chain(q, p, fin, f_r, c + 2).start()

        @pl.when(z == r)
        def _():
            for p in range(2):
                gather_piece(q, p)
                add_from(q, p, back, b_r, z < planes - 1)
                add_from(q, p, fin, f_r, z > 0)
                known = pl.ds(0, (p + 1) * hh)
                xs[q, pieces[p]] = dot3(ih[pieces[p], known], il[pieces[p], known], -fo[q, known])
                from_source(solved, q, start, (p,))

            @pl.when(k == 0)
            def _():
                for p in range(2):
                    rows = pl.ds(h + p * hh, hh)
                    s[q, rows] = s[q, rows] + dot3(lh[rows], ll[rows], xs[q])
                    exchange(q, p).start()

            @pl.when(q == c)
            def _():
                xo[mine] = xs[q]

            @pl.when(q != c)
            def _():
                deliver(q, q).start()

    yh[...], yl[...] = transposed(xs)

    @pl.loop(0, planes)
    def _(i):
        target = (z + 1 + i) % planes
        away, home = 2 * target + 1 - k, 2 * target + k
        g[away] = g[away] + dot3(yh[...], yl[...], xs[away])
        pair_up(target).start()
        g[home] = g[home] + dot3(yh[...], yl[...], xs[home])

    @pl.loop(0, planes)
    def _(i):
        target = (z + 1 + i) % planes
        pair_up(target).wait_recv()
        g[2 * target + k] = g[2 * target + k] + gx[target]

        @pl.when(target != z)
        def _():
            scatter(target, z).start()

    @pl.loop(0, nc)
    def _(q):
        for p in range(2):
            exchange(q, p).wait_send()

        sent(prior, q, q // per)
        sent(solved, q, z)

        @pl.when(z != r)
        def _():
            for p in range(2):
                chain(q, p, fin, f_r, partner).wait_send()

        @pl.when(z == r)
        def _():
            @pl.when(q != c)
            def _():
                deliver(q, partner).wait_send()

    for half in range(2):
        @pl.when(c != 2 * r + half)
        def _():
            remote(
                xs.at[0], xo.at[pl.ds(half * h, h)], o_s.at[0], o_r.at[half], (r, partner)
            ).wait_recv()

    out_ref[...] = xo[...]
    loads[4].wait()
    post_ref[...] = kq_ref[...] - g[c]

    @pl.loop(0, planes)
    def _(i):
        pair_up(i).wait_send()

        @pl.when(i != z)
        def _():
            scatter(i, z).wait_send()
            scatter((z + 1) % planes, i).wait_recv()
            post_ref[...] = post_ref[...] - gin[i]


def body(l_rows, v_prev, l_tail, k_cross, k_query):
    nr, nc = lax.axis_size("row"), lax.axis_size("col")
    tr, tc = l_tail.shape
    tm = l_rows.shape[1]
    w = k_cross.shape[1]
    assert tr == 2 * tc and nc == 2 * nr
    query = w * nc
    slots = sum(grid_of(nr)) - 2
    planes, rows = nc // 2, query // nr

    vmem = pl.BlockSpec(memory_space=pltpu.VMEM)
    return pl.pallas_call(
        functools.partial(solve_kernel, nr, nc),
        out_shape=(
            jax.ShapeDtypeStruct((tr, w), F32),
            jax.ShapeDtypeStruct(k_query.shape, F32),
        ),
        in_specs=[pl.BlockSpec(memory_space=pl.ANY)] * 5,
        out_specs=(vmem, vmem),
        scratch_shapes=[
            pltpu.VMEM(l_rows.shape, F32), pltpu.VMEM(v_prev.shape, F32), pltpu.VMEM(l_tail.shape, F32),
            pltpu.VMEM(k_cross.shape, F32), pltpu.VMEM(k_query.shape, F32),
            pltpu.VMEM((tr, tm), BF16), pltpu.VMEM((tr, tm), BF16),
            pltpu.VMEM((tr, tc), BF16), pltpu.VMEM((tr, tc), BF16),
            pltpu.VMEM((tc, tc), F32),
            pltpu.VMEM((tc, tc), BF16), pltpu.VMEM((tc, tc), BF16),
            pltpu.VMEM((rows, tm), BF16), pltpu.VMEM((rows, tm), BF16),
            pltpu.VMEM((rows, tc), BF16), pltpu.VMEM((rows, tc), BF16),
            pltpu.VMEM((nc, tr, w), F32),
        ] + [pltpu.VMEM((nc, tc, w), F32)] * 5 + [
            pltpu.VMEM((nc, tm, w), F32),
            pltpu.VMEM((tr, w), F32),
            pltpu.VMEM((nc, rows, w), F32),
            pltpu.VMEM((planes, rows, w), F32),
            pltpu.VMEM((planes, rows, w), F32),
        ] + [pltpu.SemaphoreType.DMA((2, nc))] * 5 + [
            pltpu.SemaphoreType.DMA((nc,)),
            pltpu.SemaphoreType.DMA((2,)),
        ] + [
            pltpu.SemaphoreType.DMA((slots, 2, nc)), pltpu.SemaphoreType.DMA((2, nc)),
        ] * 2 + [pltpu.SemaphoreType.DMA((planes,))] * 4 + [pltpu.SemaphoreType.DMA((5,))],
        compiler_params=pltpu.CompilerParams(
            collective_id=0, has_side_effects=True, vmem_limit_bytes=56 * 2**20
        ),
        cost_estimate=pl.CostEstimate(
            flops=12 * tr * tc * query, bytes_accessed=8 * tr * query, transcendentals=0
        ),
    )(l_rows, v_prev, l_tail, k_cross, k_query)


def solution(mesh):
    in_specs = (P("row", "col"), P("col", "row"), P("row", "col"), P("row", "col"), P("row", "col"))
    out_specs = (P("row", "col"), P("row", "col"))
    return jax.shard_map(body, mesh=mesh, in_specs=in_specs, out_specs=out_specs, check_vma=False)
```

```python
import functools

import jax
import jax.numpy as jnp
from jax import lax
from jax.experimental import pallas as pl
from jax.experimental.pallas import tpu as pltpu
from jax.sharding import PartitionSpec as P

F32 = jnp.float32
BF16 = jnp.bfloat16
MESH = pl.DeviceIdType.MESH


def split(value):
    high = value.astype(BF16)
    return high, (value - high.astype(F32)).astype(BF16)


def dot3(high, low, value):
    value_high, value_low = split(value)
    total = jnp.dot(high, value_high, preferred_element_type=F32)
    total += jnp.dot(high, value_low, preferred_element_type=F32)
    return total + jnp.dot(low, value_high, preferred_element_type=F32)


def start(copy):
    copy.start()


def wait_send(copy):
    copy.wait_send()


def grid_of(count):
    side = max(i for i in range(1, count + 1) if count % i == 0 and i * i <= count)
    return side, count // side


def exact_dot(a, b):
    return jnp.dot(a, b, precision=lax.Precision.HIGHEST, preferred_element_type=F32)


def invert(base, block_ref, out_ref):
    order = out_ref.shape[0]
    rows = lax.broadcasted_iota(jnp.int32, (base, base), 0)
    cols = lax.broadcasted_iota(jnp.int32, (base, base), 1)
    blocks = [block_ref[pl.ds(i, base), pl.ds(i, base)] for i in range(0, order, base)]
    inverses = [jnp.where(rows == cols, 1.0 / block, 0.0) for block in blocks]
    size = 1
    while size < base:
        pair = ((rows // size) % 2 == 1) & (cols // size == rows // size - 1)
        lefts = [exact_dot(inv, jnp.where(pair, block, 0.0)) for inv, block in zip(inverses, blocks)]
        inverses = [inv - exact_dot(left, inv) for inv, left in zip(inverses, lefts)]
        size *= 2
    out_ref[...] = jnp.zeros_like(out_ref)
    for i, inv in enumerate(inverses):
        out_ref[pl.ds(i * base, base), pl.ds(i * base, base)] = inv
    while size < order:
        for i in range(0, order, 2 * size):
            first, second = pl.ds(i, size), pl.ds(i + size, size)
            left = exact_dot(out_ref[second, second], block_ref[second, first])
            out_ref[second, first] = -exact_dot(left, out_ref[first, first])
        size *= 2


def solve_kernel(
    nr, nc, lr_hbm, v_hbm, lt_hbm, kc_hbm, kq_hbm, out_ref, post_ref,
    lr_ref, v_ref, lt_ref, kc_ref, kq_ref,
    rh, rl, lh, ll, inv, ih, il, th, tl, yh, yl, s, ex, fin, back, xs, fo, vs, xo, g, gx, gin,
    ex_s, ex_r, c_s, f_r, b_r, o_s, o_r, x_s, x_r, v_s, v_r, gx_s, gx_r, g_s, g_r, load_s,
):
    r, c = lax.axis_index("row"), lax.axis_index("col")
    h = xs.shape[1]
    z, k = c // 2, c % 2
    planes = nc // 2
    partner = c + 1 - 2 * k
    mine = pl.ds(pl.multiple_of(k * h, h), h)
    hh = h // 2
    pieces = [pl.ds(i * hh, hh) for i in range(2)]

    def rows_of(half, p):
        return pl.ds(pl.multiple_of(half * h + p * hh, hh), hh)

    loads = [
        pltpu.make_async_copy(src, dst, load_s.at[i])
        for i, (src, dst) in enumerate([
            (v_hbm, v_ref), (lr_hbm, lr_ref), (kc_hbm, kc_ref), (lt_hbm, lt_ref), (kq_hbm, kq_ref)
        ])
    ]
    for load in loads:
        load.start()

    barrier = pltpu.get_barrier_semaphore()

    @pl.loop(1, nr)
    def _(i):
        pl.semaphore_signal(barrier, inc=1, device_id=((r + i) % nr, c), device_id_type=MESH)

    @pl.loop(1, nc)
    def _(i):
        pl.semaphore_signal(barrier, inc=1, device_id=(r, (c + i) % nc), device_id_type=MESH)

    pl.semaphore_wait(barrier, nr + nc - 2)

    def remote(src, dst, send, recv, device):
        return pltpu.make_async_remote_copy(
            src_ref=src, dst_ref=dst, send_sem=send, recv_sem=recv, device_id=device, device_id_type=MESH
        )

    def exchange(q, p):
        return remote(
            s.at[q, rows_of(1 - k, p)], ex.at[q, pieces[p]], ex_s.at[p, q], ex_r.at[p, q], (r, partner)
        )

    def chain(q, p, dst, recv, target):
        return remote(
            fo.at[q, pieces[p]], dst.at[q, pieces[p]], c_s.at[p, q], recv.at[p, q], (r, target)
        )

    def gather_piece(q, p):
        exchange(q, p).wait_recv()
        fo[q, pieces[p]] = s[q, rows_of(k, p)] + ex[q, pieces[p]]

    def add_from(q, p, dst, recv, there):
        @pl.when(there)
        def _():
            chain(q, p, dst, recv, partner).wait_recv()
            fo[q, pieces[p]] = fo[q, pieces[p]] + dst[q, pieces[p]]

    ga, gb = grid_of(nr)
    a, b = r // gb, r % gb

    def halves(buf, sends, recvs, q, half, along, i):
        rows = buf.shape[1] // 2
        part = pl.ds(half * rows, rows)
        row, slot = (a * gb + (b + i) % gb, i - 1) if along else (((a + i) % ga) * gb + b, gb - 2 + i)
        return remote(
            buf.at[q, part], buf.at[q, part], sends.at[slot, half, q], recvs.at[half, q], (row, c)
        )

    def from_source(group, q, act, part=(0, 1)):
        for half in part:
            for i in range(1, gb):
                act(halves(*group, q, half, True, i))
            for i in range(1, ga):
                act(halves(*group, q, half, False, i))

    def pass_on(group, q, half, act):
        for i in range(1, gb if half else ga):
            act(halves(*group, q, half, bool(half), i))

    def arrived(group, q, half):
        halves(*group, q, half, gb > 1, 1).wait_recv()

    def receive(group, q, src):
        @pl.when((a == src // gb) & (b != src % gb))
        def _():
            arrived(group, q, 0)
            pass_on(group, q, 0, start)
            arrived(group, q, 1)

        @pl.when((a != src // gb) & (b == src % gb))
        def _():
            arrived(group, q, 1)
            pass_on(group, q, 1, start)
            arrived(group, q, 0)

        @pl.when((a != src // gb) & (b != src % gb))
        def _():
            arrived(group, q, 0)
            arrived(group, q, 1)

    def sent(group, q, src):
        @pl.when(r == src)
        def _():
            from_source(group, q, wait_send)

        @pl.when((a == src // gb) & (b != src % gb))
        def _():
            pass_on(group, q, 0, wait_send)

        @pl.when((a != src // gb) & (b == src % gb))
        def _():
            pass_on(group, q, 1, wait_send)

    solved, prior = (xs, x_s, x_r), (vs, v_s, v_r)
    per = nc // nr

    def turn(t):
        return (t % nr) * per + t // nr

    def deliver(q, target):
        return remote(xs.at[q], xo.at[mine], o_s.at[q], o_r.at[k], (r, target))

    def pair_up(target):
        return remote(
            g.at[2 * target + 1 - k], gx.at[target], gx_s.at[target], gx_r.at[target], (r, partner)
        )

    def scatter(target, slot):
        return remote(
            g.at[2 * target + k], gin.at[slot], g_s.at[target], g_r.at[slot], (r, 2 * target + k)
        )

    def transposed(chunks):
        return split(jnp.concatenate([chunks[r * per + i].T for i in range(per)], axis=0))

    w = kc_ref.shape[1]
    loads[0].wait()
    for i in range(per):
        vs[r * per + i] = v_ref[:, i * w:(i + 1) * w]
        from_source(prior, r * per + i, start)

    loads[1].wait()
    rh[...], rl[...] = split(lr_ref[...])
    loads[2].wait()

    @pl.loop(0, nc + 1)
    def _(t):
        @pl.when(t < nc)
        def _():
            q = turn(t)
            receive(prior, q, q // per)

            def update(half, p):
                rows = rows_of(half, p)
                term = dot3(rh[rows], rl[rows], vs[q])
                s[q, rows] = term - jnp.where(q == c, kc_ref[rows], 0.0)

            for p in range(2):
                update(1 - k, p)

                @pl.when((z > r) | ((z == r) & (k == 1)))
                def _():
                    exchange(q, p).start()

            for p in range(2):
                update(k, p)

        @pl.when((z > r) & (t > 0))
        def _():
            q = turn(t - 1)
            for p in range(2):
                gather_piece(q, p)
                add_from(q, p, back, b_r, z < planes - 1)
                chain(q, p, back, b_r, c - 2).start()

    def prior_gram():
        th[...], tl[...] = transposed(vs)

        @pl.loop(0, nc)
        def _(q):
            g[q] = dot3(th[...], tl[...], vs[q])

    loads[3].wait()

    @pl.when(z <= r)
    def _():
        lh[...], ll[...] = split(lt_ref[...])

    @pl.when(z == r)
    def _():
        for half in range(2):
            @pl.when(k == half)
            def _():
                invert(min(h, 128), lt_ref.at[pl.ds(half * h, h)], inv)

        ih[...], il[...] = split(inv[...])

    pl.when(z > 0)(prior_gram)

    @pl.loop(0, nc)
    def _(t):
        q = turn(t)
        receive(solved, q, z)

        @pl.when(z < r)
        def _():
            def update(half, p):
                rows = rows_of(half, p)
                s[q, rows] = s[q, rows] + dot3(lh[rows], ll[rows], xs[q])

            for p in range(2):
                update(1 - k, p)
                exchange(q, p).start()

            for p in range(2):
                update(k, p)
                gather_piece(q, p)
                add_from(q, p, fin, f_r, z > 0)
                chain(q, p, fin, f_r, c + 2).start()

        @pl.when(z == r)
        def _():
            for p in range(2):
                gather_piece(q, p)
                add_from(q, p, back, b_r, z < planes - 1)
                add_from(q, p, fin, f_r, z > 0)
                known = pl.ds(0, (p + 1) * hh)
                xs[q, pieces[p]] = dot3(ih[pieces[p], known], il[pieces[p], known], -fo[q, known])
                from_source(solved, q, start, (p,))

            @pl.when(k == 0)
            def _():
                for p in range(2):
                    rows = pl.ds(h + p * hh, hh)
                    s[q, rows] = s[q, rows] + dot3(lh[rows], ll[rows], xs[q])
                    exchange(q, p).start()

            @pl.when(q == c)
            def _():
                xo[mine] = xs[q]

            @pl.when(q != c)
            def _():
                deliver(q, q).start()

    pl.when(z == 0)(prior_gram)
    yh[...], yl[...] = transposed(xs)

    @pl.loop(0, planes)
    def _(i):
        target = (z + 1 + i) % planes
        away, home = 2 * target + 1 - k, 2 * target + k
        g[away] = g[away] + dot3(yh[...], yl[...], xs[away])
        pair_up(target).start()
        g[home] = g[home] + dot3(yh[...], yl[...], xs[home])

    @pl.loop(0, planes)
    def _(i):
        target = (z + 1 + i) % planes
        pair_up(target).wait_recv()
        g[2 * target + k] = g[2 * target + k] + gx[target]

        @pl.when(target != z)
        def _():
            scatter(target, z).start()

    @pl.loop(0, nc)
    def _(q):
        for p in range(2):
            exchange(q, p).wait_send()

        sent(prior, q, q // per)
        sent(solved, q, z)

        @pl.when(z != r)
        def _():
            for p in range(2):
                chain(q, p, fin, f_r, partner).wait_send()

        @pl.when(z == r)
        def _():
            @pl.when(q != c)
            def _():
                deliver(q, partner).wait_send()

    for half in range(2):
        @pl.when(c != 2 * r + half)
        def _():
            remote(
                xs.at[0], xo.at[pl.ds(half * h, h)], o_s.at[0], o_r.at[half], (r, partner)
            ).wait_recv()

    out_ref[...] = xo[...]
    loads[4].wait()
    post_ref[...] = kq_ref[...] - g[c]

    @pl.loop(0, planes)
    def _(i):
        pair_up(i).wait_send()

        @pl.when(i != z)
        def _():
            scatter(i, z).wait_send()
            scatter((z + 1) % planes, i).wait_recv()
            post_ref[...] = post_ref[...] - gin[i]


def body(l_rows, v_prev, l_tail, k_cross, k_query):
    nr, nc = lax.axis_size("row"), lax.axis_size("col")
    tr, tc = l_tail.shape
    tm = l_rows.shape[1]
    w = k_cross.shape[1]
    assert tr == 2 * tc and nc == 2 * nr
    query = w * nc
    slots = sum(grid_of(nr)) - 2
    planes, rows = nc // 2, query // nr

    vmem = pl.BlockSpec(memory_space=pltpu.VMEM)
    return pl.pallas_call(
        functools.partial(solve_kernel, nr, nc),
        out_shape=(
            jax.ShapeDtypeStruct((tr, w), F32),
            jax.ShapeDtypeStruct(k_query.shape, F32),
        ),
        in_specs=[pl.BlockSpec(memory_space=pl.ANY)] * 5,
        out_specs=(vmem, vmem),
        scratch_shapes=[
            pltpu.VMEM(l_rows.shape, F32), pltpu.VMEM(v_prev.shape, F32), pltpu.VMEM(l_tail.shape, F32),
            pltpu.VMEM(k_cross.shape, F32), pltpu.VMEM(k_query.shape, F32),
            pltpu.VMEM((tr, tm), BF16), pltpu.VMEM((tr, tm), BF16),
            pltpu.VMEM((tr, tc), BF16), pltpu.VMEM((tr, tc), BF16),
            pltpu.VMEM((tc, tc), F32),
            pltpu.VMEM((tc, tc), BF16), pltpu.VMEM((tc, tc), BF16),
            pltpu.VMEM((rows, tm), BF16), pltpu.VMEM((rows, tm), BF16),
            pltpu.VMEM((rows, tc), BF16), pltpu.VMEM((rows, tc), BF16),
            pltpu.VMEM((nc, tr, w), F32),
        ] + [pltpu.VMEM((nc, tc, w), F32)] * 5 + [
            pltpu.VMEM((nc, tm, w), F32),
            pltpu.VMEM((tr, w), F32),
            pltpu.VMEM((nc, rows, w), F32),
            pltpu.VMEM((planes, rows, w), F32),
            pltpu.VMEM((planes, rows, w), F32),
        ] + [pltpu.SemaphoreType.DMA((2, nc))] * 5 + [
            pltpu.SemaphoreType.DMA((nc,)),
            pltpu.SemaphoreType.DMA((2,)),
        ] + [
            pltpu.SemaphoreType.DMA((slots, 2, nc)), pltpu.SemaphoreType.DMA((2, nc)),
        ] * 2 + [pltpu.SemaphoreType.DMA((planes,))] * 4 + [pltpu.SemaphoreType.DMA((5,))],
        compiler_params=pltpu.CompilerParams(
            collective_id=0, has_side_effects=True, vmem_limit_bytes=56 * 2**20
        ),
        cost_estimate=pl.CostEstimate(
            flops=12 * tr * tc * query, bytes_accessed=8 * tr * query, transcendentals=0
        ),
    )(l_rows, v_prev, l_tail, k_cross, k_query)


def solution(mesh):
    in_specs = (P("row", "col"), P("col", "row"), P("row", "col"), P("row", "col"), P("row", "col"))
    out_specs = (P("row", "col"), P("row", "col"))
    return jax.shard_map(body, mesh=mesh, in_specs=in_specs, out_specs=out_specs, check_vma=False)
```

```python
import functools

import jax
import jax.numpy as jnp
from jax import lax
from jax.experimental import pallas as pl
from jax.experimental.pallas import tpu as pltpu
from jax.sharding import PartitionSpec as P

F32 = jnp.float32
BF16 = jnp.bfloat16
MESH = pl.DeviceIdType.MESH


def split(value):
    high = value.astype(BF16)
    return high, (value - high.astype(F32)).astype(BF16)


def dot3(high, low, value):
    value_high, value_low = split(value)
    total = jnp.dot(high, value_high, preferred_element_type=F32)
    total += jnp.dot(high, value_low, preferred_element_type=F32)
    return total + jnp.dot(low, value_high, preferred_element_type=F32)


def start(copy):
    copy.start()


def wait_send(copy):
    copy.wait_send()


def grid_of(count):
    side = max(i for i in range(1, count + 1) if count % i == 0 and i * i <= count)
    return side, count // side


def exact_dot(a, b):
    return jnp.dot(a, b, precision=lax.Precision.HIGHEST, preferred_element_type=F32)


def invert(base, block_ref, out_ref):
    order = out_ref.shape[0]
    rows = lax.broadcasted_iota(jnp.int32, (base, base), 0)
    cols = lax.broadcasted_iota(jnp.int32, (base, base), 1)
    blocks = [block_ref[pl.ds(i, base), pl.ds(i, base)] for i in range(0, order, base)]
    inverses = [jnp.where(rows == cols, 1.0 / block, 0.0) for block in blocks]
    size = 1
    while size < base:
        pair = ((rows // size) % 2 == 1) & (cols // size == rows // size - 1)
        lefts = [exact_dot(inv, jnp.where(pair, block, 0.0)) for inv, block in zip(inverses, blocks)]
        inverses = [inv - exact_dot(left, inv) for inv, left in zip(inverses, lefts)]
        size *= 2
    out_ref[...] = jnp.zeros_like(out_ref)
    for i, inv in enumerate(inverses):
        out_ref[pl.ds(i * base, base), pl.ds(i * base, base)] = inv
    while size < order:
        for i in range(0, order, 2 * size):
            first, second = pl.ds(i, size), pl.ds(i + size, size)
            left = exact_dot(out_ref[second, second], block_ref[second, first])
            out_ref[second, first] = -exact_dot(left, out_ref[first, first])
        size *= 2


def solve_kernel(
    nr, nc, lr_hbm, v_hbm, lt_hbm, kc_hbm, kq_hbm, out_ref, post_ref,
    lr_ref, v_ref, lt_ref, kc_ref, kq_ref,
    rh, rl, lh, ll, inv, ih, il, th, tl, yh, yl, s, ex, fin, back, xs, fo, vs, xo, g, gx, gin,
    ex_s, ex_r, c_s, f_r, b_r, o_s, o_r, x_s, x_r, v_s, v_r, gx_s, gx_r, g_s, g_r, load_s,
):
    r, c = lax.axis_index("row"), lax.axis_index("col")
    h = xs.shape[1]
    z, k = c // 2, c % 2
    planes = nc // 2
    partner = c + 1 - 2 * k
    mine = pl.ds(pl.multiple_of(k * h, h), h)
    hh = h // 2
    pieces = [pl.ds(i * hh, hh) for i in range(2)]

    def rows_of(half, p):
        return pl.ds(pl.multiple_of(half * h + p * hh, hh), hh)

    loads = [
        pltpu.make_async_copy(src, dst, load_s.at[i])
        for i, (src, dst) in enumerate([
            (v_hbm, v_ref), (lr_hbm, lr_ref), (kc_hbm, kc_ref), (lt_hbm, lt_ref), (kq_hbm, kq_ref)
        ])
    ]
    for load in loads:
        load.start()

    barrier = pltpu.get_barrier_semaphore()

    @pl.loop(1, nr)
    def _(i):
        pl.semaphore_signal(barrier, inc=1, device_id=((r + i) % nr, c), device_id_type=MESH)

    @pl.loop(1, nc)
    def _(i):
        pl.semaphore_signal(barrier, inc=1, device_id=(r, (c + i) % nc), device_id_type=MESH)

    pl.semaphore_wait(barrier, nr + nc - 2)

    def remote(src, dst, send, recv, device):
        return pltpu.make_async_remote_copy(
            src_ref=src, dst_ref=dst, send_sem=send, recv_sem=recv, device_id=device, device_id_type=MESH
        )

    def exchange(q, p):
        return remote(
            s.at[q, rows_of(1 - k, p)], ex.at[q, pieces[p]], ex_s.at[p, q], ex_r.at[p, q], (r, partner)
        )

    def chain(q, p, dst, recv, target):
        return remote(
            fo.at[q, pieces[p]], dst.at[q, pieces[p]], c_s.at[p, q], recv.at[p, q], (r, target)
        )

    def gather_piece(q, p):
        exchange(q, p).wait_recv()
        fo[q, pieces[p]] = s[q, rows_of(k, p)] + ex[q, pieces[p]]

    def add_from(q, p, dst, recv, there):
        @pl.when(there)
        def _():
            chain(q, p, dst, recv, partner).wait_recv()
            fo[q, pieces[p]] = fo[q, pieces[p]] + dst[q, pieces[p]]

    ga, gb = grid_of(nr)
    a, b = r // gb, r % gb

    def halves(buf, sends, recvs, q, half, along, i):
        rows = buf.shape[1] // 2
        part = pl.ds(half * rows, rows)
        row, slot = (a * gb + (b + i) % gb, i - 1) if along else (((a + i) % ga) * gb + b, gb - 2 + i)
        return remote(
            buf.at[q, part], buf.at[q, part], sends.at[slot, half, q], recvs.at[half, q], (row, c)
        )

    def from_source(group, q, act, part=(0, 1)):
        for half in part:
            for i in range(1, gb):
                act(halves(*group, q, half, True, i))
            for i in range(1, ga):
                act(halves(*group, q, half, False, i))

    def pass_on(group, q, half, act):
        for i in range(1, gb if half else ga):
            act(halves(*group, q, half, bool(half), i))

    def arrived(group, q, half):
        halves(*group, q, half, gb > 1, 1).wait_recv()

    def receive(group, q, src):
        @pl.when((a == src // gb) & (b != src % gb))
        def _():
            arrived(group, q, 0)
            pass_on(group, q, 0, start)
            arrived(group, q, 1)

        @pl.when((a != src // gb) & (b == src % gb))
        def _():
            arrived(group, q, 1)
            pass_on(group, q, 1, start)
            arrived(group, q, 0)

        @pl.when((a != src // gb) & (b != src % gb))
        def _():
            arrived(group, q, 0)
            arrived(group, q, 1)

    def sent(group, q, src):
        @pl.when(r == src)
        def _():
            from_source(group, q, wait_send)

        @pl.when((a == src // gb) & (b != src % gb))
        def _():
            pass_on(group, q, 0, wait_send)

        @pl.when((a != src // gb) & (b == src % gb))
        def _():
            pass_on(group, q, 1, wait_send)

    solved, prior = (xs, x_s, x_r), (vs, v_s, v_r)
    per = nc // nr

    def turn(t):
        return (t % nr) * per + t // nr

    def deliver(q, target):
        return remote(xs.at[q], xo.at[mine], o_s.at[q], o_r.at[k], (r, target))

    def pair_up(target):
        return remote(
            g.at[2 * target + 1 - k], gx.at[target], gx_s.at[target], gx_r.at[target], (r, partner)
        )

    def scatter(target, slot):
        return remote(
            g.at[2 * target + k], gin.at[slot], g_s.at[target], g_r.at[slot], (r, 2 * target + k)
        )

    def transposed(chunks):
        return split(jnp.concatenate([chunks[r * per + i].T for i in range(per)], axis=0))

    w = kc_ref.shape[1]
    loads[0].wait()
    for i in range(per):
        vs[r * per + i] = v_ref[:, i * w:(i + 1) * w]
        from_source(prior, r * per + i, start)

    loads[1].wait()
    rh[...], rl[...] = split(lr_ref[...])
    loads[2].wait()

    @pl.loop(0, nc + 1)
    def _(t):
        @pl.when(t < nc)
        def _():
            q = turn(t)
            receive(prior, q, q // per)

            def update(half, p):
                rows = rows_of(half, p)
                term = dot3(rh[rows], rl[rows], vs[q])
                s[q, rows] = term - jnp.where(q == c, kc_ref[rows], 0.0)

            for p in range(2):
                update(1 - k, p)

                @pl.when((z > r) | ((z == r) & (k == 1)))
                def _():
                    exchange(q, p).start()

            for p in range(2):
                update(k, p)

        @pl.when((z > r) & (t > 0))
        def _():
            q = turn(t - 1)
            for p in range(2):
                gather_piece(q, p)
                add_from(q, p, back, b_r, z < planes - 1)
                chain(q, p, back, b_r, c - 2).start()

    def prior_gram():
        th[...], tl[...] = transposed(vs)

        @pl.loop(0, nc)
        def _(q):
            g[q] = dot3(th[...], tl[...], vs[q])

    def tail_gram(first, last):
        yh[...], yl[...] = transposed(xs)

        @pl.loop(first, last)
        def _(i):
            target = (z + 1 + i) % planes
            away, home = 2 * target + 1 - k, 2 * target + k
            g[away] = g[away] + dot3(yh[...], yl[...], xs[away])
            pair_up(target).start()
            g[home] = g[home] + dot3(yh[...], yl[...], xs[home])

        @pl.loop(first, last)
        def _(i):
            target = (z + 1 + i) % planes
            pair_up(target).wait_recv()
            g[2 * target + k] = g[2 * target + k] + gx[target]

            @pl.when(target != z)
            def _():
                scatter(target, z).start()

    early = (z == planes - 1) & (r < nr - 1)

    loads[3].wait()

    @pl.when(z <= r)
    def _():
        lh[...], ll[...] = split(lt_ref[...])

    @pl.when(z == r)
    def _():
        for half in range(2):
            @pl.when(k == half)
            def _():
                invert(min(h, 128), lt_ref.at[pl.ds(half * h, h)], inv)

        ih[...], il[...] = split(inv[...])

    pl.when(z > 0)(prior_gram)

    @pl.loop(0, nc)
    def _(t):
        q = turn(t)

        @pl.when(early & (t == nc - 1))
        def _():
            tail_gram(0, planes - 1)

        receive(solved, q, z)

        @pl.when(z < r)
        def _():
            def update(half, p):
                rows = rows_of(half, p)
                s[q, rows] = s[q, rows] + dot3(lh[rows], ll[rows], xs[q])

            for p in range(2):
                update(1 - k, p)
                exchange(q, p).start()

            for p in range(2):
                update(k, p)
                gather_piece(q, p)
                add_from(q, p, fin, f_r, z > 0)
                chain(q, p, fin, f_r, c + 2).start()

        @pl.when(z == r)
        def _():
            for p in range(2):
                gather_piece(q, p)
                add_from(q, p, back, b_r, z < planes - 1)
                add_from(q, p, fin, f_r, z > 0)
                known = pl.ds(0, (p + 1) * hh)
                xs[q, pieces[p]] = dot3(ih[pieces[p], known], il[pieces[p], known], -fo[q, known])
                from_source(solved, q, start, (p,))

            @pl.when(k == 0)
            def _():
                for p in range(2):
                    rows = pl.ds(h + p * hh, hh)
                    s[q, rows] = s[q, rows] + dot3(lh[rows], ll[rows], xs[q])
                    exchange(q, p).start()

            @pl.when(q == c)
            def _():
                xo[mine] = xs[q]

            @pl.when(q != c)
            def _():
                deliver(q, q).start()

    pl.when(z == 0)(prior_gram)
    tail_gram(jnp.where(early, planes - 1, 0), planes)

    @pl.loop(0, nc)
    def _(q):
        for p in range(2):
            exchange(q, p).wait_send()

        sent(prior, q, q // per)
        sent(solved, q, z)

        @pl.when(z != r)
        def _():
            for p in range(2):
                chain(q, p, fin, f_r, partner).wait_send()

        @pl.when(z == r)
        def _():
            @pl.when(q != c)
            def _():
                deliver(q, partner).wait_send()

    for half in range(2):
        @pl.when(c != 2 * r + half)
        def _():
            remote(
                xs.at[0], xo.at[pl.ds(half * h, h)], o_s.at[0], o_r.at[half], (r, partner)
            ).wait_recv()

    out_ref[...] = xo[...]
    loads[4].wait()
    post_ref[...] = kq_ref[...] - g[c]

    @pl.loop(0, planes)
    def _(i):
        pair_up(i).wait_send()

        @pl.when(i != z)
        def _():
            scatter(i, z).wait_send()
            scatter((z + 1) % planes, i).wait_recv()
            post_ref[...] = post_ref[...] - gin[i]


def body(l_rows, v_prev, l_tail, k_cross, k_query):
    nr, nc = lax.axis_size("row"), lax.axis_size("col")
    tr, tc = l_tail.shape
    tm = l_rows.shape[1]
    w = k_cross.shape[1]
    assert tr == 2 * tc and nc == 2 * nr
    query = w * nc
    slots = sum(grid_of(nr)) - 2
    planes, rows = nc // 2, query // nr

    vmem = pl.BlockSpec(memory_space=pltpu.VMEM)
    return pl.pallas_call(
        functools.partial(solve_kernel, nr, nc),
        out_shape=(
            jax.ShapeDtypeStruct((tr, w), F32),
            jax.ShapeDtypeStruct(k_query.shape, F32),
        ),
        in_specs=[pl.BlockSpec(memory_space=pl.ANY)] * 5,
        out_specs=(vmem, vmem),
        scratch_shapes=[
            pltpu.VMEM(l_rows.shape, F32), pltpu.VMEM(v_prev.shape, F32), pltpu.VMEM(l_tail.shape, F32),
            pltpu.VMEM(k_cross.shape, F32), pltpu.VMEM(k_query.shape, F32),
            pltpu.VMEM((tr, tm), BF16), pltpu.VMEM((tr, tm), BF16),
            pltpu.VMEM((tr, tc), BF16), pltpu.VMEM((tr, tc), BF16),
            pltpu.VMEM((tc, tc), F32),
            pltpu.VMEM((tc, tc), BF16), pltpu.VMEM((tc, tc), BF16),
            pltpu.VMEM((rows, tm), BF16), pltpu.VMEM((rows, tm), BF16),
            pltpu.VMEM((rows, tc), BF16), pltpu.VMEM((rows, tc), BF16),
            pltpu.VMEM((nc, tr, w), F32),
        ] + [pltpu.VMEM((nc, tc, w), F32)] * 5 + [
            pltpu.VMEM((nc, tm, w), F32),
            pltpu.VMEM((tr, w), F32),
            pltpu.VMEM((nc, rows, w), F32),
            pltpu.VMEM((planes, rows, w), F32),
            pltpu.VMEM((planes, rows, w), F32),
        ] + [pltpu.SemaphoreType.DMA((2, nc))] * 5 + [
            pltpu.SemaphoreType.DMA((nc,)),
            pltpu.SemaphoreType.DMA((2,)),
        ] + [
            pltpu.SemaphoreType.DMA((slots, 2, nc)), pltpu.SemaphoreType.DMA((2, nc)),
        ] * 2 + [pltpu.SemaphoreType.DMA((planes,))] * 4 + [pltpu.SemaphoreType.DMA((5,))],
        compiler_params=pltpu.CompilerParams(
            collective_id=0, has_side_effects=True, vmem_limit_bytes=56 * 2**20
        ),
        cost_estimate=pl.CostEstimate(
            flops=12 * tr * tc * query, bytes_accessed=8 * tr * query, transcendentals=0
        ),
    )(l_rows, v_prev, l_tail, k_cross, k_query)


def solution(mesh):
    in_specs = (P("row", "col"), P("col", "row"), P("row", "col"), P("row", "col"), P("row", "col"))
    out_specs = (P("row", "col"), P("row", "col"))
    return jax.shard_map(body, mesh=mesh, in_specs=in_specs, out_specs=out_specs, check_vma=False)
```
